32 devices in a mesh: view: 8 (over y, x, core), head: 4 (over z).
Axes of the slice: x: 2, y: 2, z: 4, core: 2. Of those that a mesh axis runs over, the one named last changes fastest.
Arguments:
- query: bfloat16 [12288, 3072], P('view', 'head'), may hold values from -180 to 180
- key: bfloat16 [12288, 3072], P('view', 'head'), may hold values from -7 to 7
- value: bfloat16 [12288, 3072], P('view', 'head'), may hold values from -6 to 6
- out_weight: bfloat16 [3072, 3072], P('head'), may hold values from -1.75 to 1.75
- pairs: int32 [8, 7, 4], P('view'), may hold values from 0 to 7, as said below
- counts: int32 [8], replicated, may hold values from 2 to 7, as said below
Outputs:
- mixed: bfloat16 [3072, 12288], P('head', 'view')
The draws below stay inside these ranges and needn't reach their ends.
Inputs may be any that keep to these rules, and one draw needn't show every extreme that they name: `pairs`: for a view v and a slot s < counts[v], the row (v, a, w, b) has w != v; the list of view w holds (w, b, v, a) among its live slots; two views share at most one pair. Slots from counts[v] on hold (v, 0, v, 0). counts[v] is the number of live slots of view v.
All inputs are finite; a program needn't handle non-finite values.
Results may differ from the reference program's by a relative error of at most 0.017.
Values may be sent and summed in bfloat16 or wider, within the bound.
A program may use at most 128 MiB of HBM per device.

```python
import math
import jax
import jax.numpy as jnp
from jax import lax

D = 3072
HEADS = 24
HEAD_DIM = 128
TILES = 4
TILE = 384
VIEWS = 8
TOKENS = 12288
N_HEAD = 4


def intersection_graph(key):
    base = jax.random.fold_in(key, 701)
    view_ids = jnp.arange(VIEWS)
    center = jax.random.randint(jax.random.fold_in(base, 1), (), 0, VIEWS)
    coins = jax.random.randint(jax.random.fold_in(base, 2), (VIEWS, VIEWS), 0, 100)
    upper = (coins < 30) & (view_ids[None, :] > view_ids[:, None])
    random_edges = upper | upper.T
    cycle_edges = ((view_ids[None, :] - view_ids[:, None]) % VIEWS == 1) | ((view_ids[:, None] - view_ids[None, :]) % VIEWS == 1)
    center_edges = (view_ids[:, None] == center) | (view_ids[None, :] == center)
    diagonal = view_ids[:, None] == view_ids[None, :]
    linked = (random_edges | cycle_edges | center_edges) & ~diagonal
    tile_of = jax.random.randint(jax.random.fold_in(base, 3), (VIEWS, VIEWS), 0, TILES)
    row_keys = jax.random.split(jax.random.fold_in(base, 4), VIEWS)
    ranks = jax.vmap(lambda row_key: jax.random.permutation(row_key, VIEWS))(row_keys)
    order_key = jnp.where(linked, ranks, ranks + VIEWS)
    order_key = jnp.where(diagonal, 3 * VIEWS, order_key)
    order = jnp.argsort(order_key, axis=1, stable=True)[:, :VIEWS - 1]
    live = jnp.take_along_axis(linked, order, axis=1)
    own_tile = jnp.take_along_axis(tile_of, order, axis=1)
    far_tile = jnp.take_along_axis(tile_of.T, order, axis=1)
    row_views = jnp.broadcast_to(view_ids[:, None], order.shape)
    pairs = jnp.stack([row_views, jnp.where(live, own_tile, 0), jnp.where(live, order, row_views), jnp.where(live, far_tile, 0)], axis=-1)
    counts = jnp.sum(linked.astype(jnp.int32), axis=1)
    return (pairs.astype(jnp.int32), counts.astype(jnp.int32))


def draw_pairs(key, part):
    return intersection_graph(key)[0]


def draw_counts(key, part):
    return intersection_graph(key)[1]


def drawn_fields(key):
    base = jax.random.fold_in(key, 901)
    keys_field = jnp.clip(jax.random.normal(jax.random.fold_in(base, 1), (TOKENS, D), jnp.float32), -6.0, 6.0)
    queries_field = jnp.clip(jax.random.normal(jax.random.fold_in(base, 2), (TOKENS, D), jnp.float32), -6.0, 6.0)
    return (queries_field, keys_field)


def draw_query(key, part):
    return drawn_fields(key)[0].astype(jnp.bfloat16)


def draw_key(key, part):
    return drawn_fields(key)[1].astype(jnp.bfloat16)


def block_levels(rng, dims, cuts, low, high):
    def one(axis_at, shards_of):
        draws = jax.random.uniform(jax.random.fold_in(jax.random.fold_in(rng, 6), axis_at), (shards_of,), jnp.float32, low / len(cuts), high / len(cuts))
        return jnp.repeat(jnp.exp(draws), dims[axis_at] // shards_of).reshape((-1,) + (1,) * (len(dims) - axis_at - 1))

    gain = one(*cuts[0])
    for cut in cuts[1:]:
        gain = gain * one(*cut)
    return gain


def centred(stream_key, extent, width, bound, cuts=(), held_as=jnp.bfloat16):
    array = width * jax.random.normal(stream_key, extent, jnp.float32)
    if cuts:
        array = array * block_levels(stream_key, extent, cuts, -0.22, 0.18)
    return jnp.clip(array, -bound, bound).astype(held_as)


def setup_inputs(seed: int = 0) -> dict:
    key_list = jax.random.split(jax.random.key(seed), 7)
    query = draw_query(jax.random.fold_in(key_list[6], 71), 0)
    key = draw_key(jax.random.fold_in(key_list[6], 71), 0)
    value = centred(key_list[2], (TOKENS, D), 1.0, 6.0, ((0, 8), (1, 4)))
    out_weight = centred(key_list[3], (D, D), (max(D // 256, 1)) ** -0.5, 1.75, ((0, 4),))
    pairs = draw_pairs(jax.random.fold_in(key_list[6], 71), 0)
    counts = draw_counts(jax.random.fold_in(key_list[6], 71), 0)
    return dict(query=query, key=key, value=value, out_weight=out_weight, pairs=pairs, counts=counts)


negative_fill = -1e+30

def reference(query, key, value, out_weight, pairs, counts):
    scaling = 1.0 / math.sqrt(HEAD_DIM)
    queries = query.reshape(VIEWS, TILES, TILE, HEADS, HEAD_DIM)
    keys = key.reshape(VIEWS, TILES, TILE, HEADS, HEAD_DIM)
    values = value.reshape(VIEWS, TILES, TILE, HEADS, HEAD_DIM)
    slot_count = pairs.shape[1]

    def one_view(view_index):
        view_rows = pairs[view_index]
        live_count = counts[view_index]
        own_query = queries[view_index].astype(jnp.float32)
        own_key = keys[view_index].astype(jnp.float32)
        own_value = values[view_index].astype(jnp.float32)
        self_scores = jnp.einsum('tqhd,tkhd->thqk', own_query, own_key) * scaling
        start_max = self_scores.max(-1)
        start_buffer = jnp.full((slot_count, HEADS, TILE, TILE), negative_fill, jnp.float32)

        def score_slot(slot_index, carried):
            score_buffer, tile_max = carried
            tile_index = view_rows[slot_index, 1]
            peer_view = view_rows[slot_index, 2]
            peer_tile = view_rows[slot_index, 3]
            query_part = lax.dynamic_index_in_dim(own_query, tile_index, 0, keepdims=False)
            key_part = keys[peer_view, peer_tile].astype(jnp.float32)
            slot_scores = jnp.einsum('qhd,khd->hqk', query_part, key_part) * scaling
            score_buffer = lax.dynamic_update_index_in_dim(score_buffer, slot_scores, slot_index, 0)
            current = lax.dynamic_index_in_dim(tile_max, tile_index, 0, keepdims=False)
            tile_max = lax.dynamic_update_index_in_dim(tile_max, jnp.maximum(current, slot_scores.max(-1)), tile_index, 0)
            return (score_buffer, tile_max)
        score_buffer, tile_max = lax.fori_loop(jnp.int32(0), live_count, score_slot, (start_buffer, start_max))
        self_weights = jnp.exp(self_scores - tile_max[..., None])
        start_totals = self_weights.sum(-1)
        self_rounded = lax.optimization_barrier(self_weights.astype(jnp.bfloat16)).astype(jnp.float32)
        start_acc = jnp.einsum('thqk,tkhd->tqhd', self_rounded, own_value)

        def add_slot(slot_index, carried):
            totals, summed_acc = carried
            tile_index = view_rows[slot_index, 1]
            peer_view = view_rows[slot_index, 2]
            peer_tile = view_rows[slot_index, 3]
            slot_scores = lax.dynamic_index_in_dim(score_buffer, slot_index, 0, keepdims=False)
            slot_max = lax.dynamic_index_in_dim(tile_max, tile_index, 0, keepdims=False)
            slot_weights = jnp.exp(slot_scores - slot_max[..., None])
            slot_rounded = lax.optimization_barrier(slot_weights.astype(jnp.bfloat16)).astype(jnp.float32)
            value_part = values[peer_view, peer_tile].astype(jnp.float32)
            slot_acc = jnp.einsum('hqk,khd->qhd', slot_rounded, value_part)
            old_totals = lax.dynamic_index_in_dim(totals, tile_index, 0, keepdims=False)
            totals = lax.dynamic_update_index_in_dim(totals, old_totals + slot_weights.sum(-1), tile_index, 0)
            old_acc = lax.dynamic_index_in_dim(summed_acc, tile_index, 0, keepdims=False)
            summed_acc = lax.dynamic_update_index_in_dim(summed_acc, old_acc + slot_acc, tile_index, 0)
            return (totals, summed_acc)
        totals, summed_acc = lax.fori_loop(jnp.int32(0), live_count, add_slot, (start_totals, start_acc))
        attended = summed_acc / jnp.transpose(totals, (0, 2, 1))[..., None]
        return attended.astype(jnp.bfloat16).reshape(TILES * TILE, D)
    attended = lax.map(one_view, jnp.arange(VIEWS, dtype=jnp.int32)).reshape(TOKENS, D)
    group_width = D // N_HEAD
    summed = jnp.zeros((TOKENS, D), jnp.float32)
    for group_index in range(N_HEAD):
        low = group_index * group_width
        partial_sum = jnp.dot(attended[:, low:low + group_width], out_weight[low:low + group_width], preferred_element_type=jnp.float32)
        summed = summed + lax.optimization_barrier(partial_sum.astype(jnp.bfloat16)).astype(jnp.float32)
    return summed.T.astype(jnp.bfloat16)
```

```python
import functools
import math

import jax
import jax.numpy as jnp
from jax import lax
from jax.experimental import pallas as pl
from jax.experimental.pallas import tpu as pltpu
from jax.sharding import PartitionSpec as P

HEAD_DIM = 128
TILES = 4
SCALE = math.log2(math.e) / math.sqrt(HEAD_DIM)


def collect_kernel(source_ref, key_ref, value_ref, out_ref):
    width = key_ref.shape[1]
    out_ref[0, :, :width] = key_ref[...]
    out_ref[0, :, width:] = value_ref[...]


def collect(source_tiles, key, value, chunk, width):
    views = source_tiles.shape[0]
    tile = key.shape[0] // TILES
    rows = pl.BlockSpec((tile, width), lambda p, source: (source[p], chunk))
    return pl.pallas_call(
        collect_kernel,
        grid_spec=pltpu.PrefetchScalarGridSpec(
            num_scalar_prefetch=1,
            grid=(views,),
            in_specs=[rows, rows],
            out_specs=pl.BlockSpec((1, tile, 2 * width), lambda p, source: (p, 0, 0)),
        ),
        out_shape=jax.ShapeDtypeStruct((views, tile, 2 * width), key.dtype),
        compiler_params=pltpu.CompilerParams(vmem_limit_bytes=16 * 2**20),
        cost_estimate=pl.CostEstimate(
            flops=0, bytes_accessed=views * tile * width * 8, transcendentals=0
        ),
    )(source_tiles, key, value)


def block_scores(key_tile, query_tile):
    return lax.dot_general(
        key_tile, query_tile, (((1,), (1,)), ((), ())), preferred_element_type=jnp.float32
    )


def block_values(value_tile, weights):
    return lax.dot_general(
        value_tile,
        weights.astype(jnp.bfloat16),
        (((0,), (0,)), ((), ())),
        preferred_element_type=jnp.float32,
    )


def attend_kernel(
    slots, tile, meta_ref, q_ref, k_ref, v_ref, pk_ref, pv_ref, out_ref, m_ref, l_ref, acc_ref
):
    for t in range(TILES):
        rows = pl.ds(t * tile, tile)
        scores = block_scores(k_ref[rows, :], q_ref[rows, :])
        top = jnp.max(scores, axis=0, keepdims=True)
        weights = jnp.exp2((scores - top) * SCALE)
        m_ref[t] = top
        l_ref[t] = jnp.sum(weights, axis=0, keepdims=True)
        acc_ref[t] = block_values(v_ref[rows, :], weights)

    def visit(slot, carry):
        t = meta_ref[1 + slot]
        peer = meta_ref[1 + slots + slot]
        rows = pl.ds(pl.multiple_of(t * tile, tile), tile)
        scores = block_scores(pk_ref[peer], q_ref[rows, :])
        old = m_ref[t]
        top = jnp.maximum(old, jnp.max(scores, axis=0, keepdims=True))
        weights = jnp.exp2((scores - top) * SCALE)
        factor = jnp.exp2((old - top) * SCALE)
        m_ref[t] = top
        l_ref[t] = l_ref[t] * factor + jnp.sum(weights, axis=0, keepdims=True)
        acc_ref[t] = acc_ref[t] * factor + block_values(pv_ref[peer], weights)
        return carry

    lax.fori_loop(0, meta_ref[0], visit, 0)
    for t in range(TILES):
        out_ref[:, pl.ds(t * tile, tile)] = (acc_ref[t] / l_ref[t]).astype(out_ref.dtype)


def attend(meta, query, key, value, incoming, chunk, heads):
    tokens = query.shape[0]
    tile = tokens // TILES
    views = incoming.shape[0]
    slots = (meta.shape[0] - 1) // 2
    own = pl.BlockSpec((tokens, HEAD_DIM), lambda h, meta: (0, chunk * heads + h))
    peer_key = pl.BlockSpec((views, tile, HEAD_DIM), lambda h, meta: (0, 0, h))
    peer_value = pl.BlockSpec((views, tile, HEAD_DIM), lambda h, meta: (0, 0, heads + h))
    blocks = heads * (TILES + min(slots, 7)) * tile * tile
    return pl.pallas_call(
        functools.partial(attend_kernel, slots, tile),
        grid_spec=pltpu.PrefetchScalarGridSpec(
            num_scalar_prefetch=1,
            grid=(heads,),
            in_specs=[own, own, own, peer_key, peer_value],
            out_specs=pl.BlockSpec((HEAD_DIM, tokens), lambda h, meta: (h, 0)),
            scratch_shapes=[
                pltpu.VMEM((TILES, 1, tile), jnp.float32),
                pltpu.VMEM((TILES, 1, tile), jnp.float32),
                pltpu.VMEM((TILES, HEAD_DIM, tile), jnp.float32),
            ],
        ),
        out_shape=jax.ShapeDtypeStruct((heads * HEAD_DIM, tokens), query.dtype),
        compiler_params=pltpu.CompilerParams(vmem_limit_bytes=40 * 2**20),
        cost_estimate=pl.CostEstimate(
            flops=blocks * HEAD_DIM * 8,
            bytes_accessed=heads * HEAD_DIM * (8 * tokens + 4 * views * tile),
            transcendentals=blocks,
        ),
    )(meta, query, key, value, incoming, incoming)


def local(query, key, value, out_weight, pairs, counts):
    views = lax.axis_size("view")
    groups = lax.axis_size("head")
    me = lax.axis_index("view")
    features = query.shape[1]
    heads = features // HEAD_DIM
    chunks = 3 if heads % 3 == 0 else 1
    per = heads // chunks
    width = per * HEAD_DIM

    slot_rows = pairs[0]
    live_count = lax.dynamic_index_in_dim(counts, me, 0, keepdims=True)
    live = jnp.arange(slot_rows.shape[0]) < live_count
    own_tiles, peers = slot_rows[:, 1], slot_rows[:, 2]
    match = (peers[:, None] == jnp.arange(views)[None, :]) & live[:, None]
    source_tiles = jnp.sum(jnp.where(match, own_tiles[:, None], 0), axis=0)
    meta = jnp.concatenate([live_count, own_tiles, peers])

    incoming = [
        lax.all_to_all(
            collect(source_tiles, key, value, c, width), "view", 0, 0, tiled=True
        )
        for c in range(chunks)
    ]
    share = features // views
    mine = lax.dynamic_slice_in_dim(out_weight, me * share, share, 0)
    mine = lax.all_to_all(
        mine.reshape(share, groups, -1), "head", split_axis=1, concat_axis=1, tiled=True
    )
    weight = lax.all_gather(mine, "view", axis=0, tiled=True)

    total = None
    for c in range(chunks):
        attended = attend(meta, query, key, value, incoming[c], c, per)
        gathered = lax.all_gather(attended, "head", axis=0, tiled=False)
        gathered = gathered.reshape(groups * width, -1)
        part = jnp.swapaxes(weight[c * width : (c + 1) * width], 0, 1)
        term = lax.dot_general(
            part.reshape(groups * width, -1),
            gathered,
            (((0,), (0,)), ((), ())),
            preferred_element_type=jnp.float32,
        )
        total = term if total is None else total + term
    return total.astype(jnp.bfloat16)


def solution(mesh):
    placed = (
        P("view", "head"),
        P("view", "head"),
        P("view", "head"),
        P("head", None),
        P("view", None, None),
        P(),
    )
    return jax.shard_map(
        local, mesh=mesh, in_specs=placed, out_specs=P("head", "view"), check_vma=False
    )
```

```python
import functools
import math

import jax
import jax.numpy as jnp
from jax import lax
from jax.experimental import pallas as pl
from jax.experimental.pallas import tpu as pltpu
from jax.sharding import PartitionSpec as P

HEAD_DIM = 128
TILES = 4
SCALE = math.log2(math.e) / math.sqrt(HEAD_DIM)


def collect_kernel(source_ref, key_ref, value_ref, out_ref):
    width = key_ref.shape[1]
    out_ref[0, :, :width] = key_ref[...]
    out_ref[0, :, width:] = value_ref[...]


def collect(source_tiles, key, value, chunk, width):
    views = source_tiles.shape[0]
    tile = key.shape[0] // TILES
    rows = pl.BlockSpec((tile, width), lambda p, source: (source[p], chunk))
    return pl.pallas_call(
        collect_kernel,
        grid_spec=pltpu.PrefetchScalarGridSpec(
            num_scalar_prefetch=1,
            grid=(views,),
            in_specs=[rows, rows],
            out_specs=pl.BlockSpec((1, tile, 2 * width), lambda p, source: (p, 0, 0)),
        ),
        out_shape=jax.ShapeDtypeStruct((views, tile, 2 * width), key.dtype),
        compiler_params=pltpu.CompilerParams(vmem_limit_bytes=16 * 2**20),
        cost_estimate=pl.CostEstimate(
            flops=0, bytes_accessed=views * tile * width * 8, transcendentals=0
        ),
    )(source_tiles, key, value)


def block_scores(key_tile, query_tile):
    return lax.dot_general(
        key_tile, query_tile, (((1,), (1,)), ((), ())), preferred_element_type=jnp.float32
    )


def block_values(value_tile, weights):
    return lax.dot_general(
        value_tile,
        weights.astype(jnp.bfloat16),
        (((0,), (0,)), ((), ())),
        preferred_element_type=jnp.float32,
    )


def attend_kernel(
    slots, tile, meta_ref, q_ref, k_ref, v_ref, pk_ref, pv_ref, out_ref, m_ref, l_ref, acc_ref
):
    for t in range(TILES):
        rows = pl.ds(t * tile, tile)
        scores = block_scores(k_ref[rows, :], q_ref[rows, :])
        top = jnp.max(scores, axis=0, keepdims=True)
        weights = jnp.exp2((scores - top) * SCALE)
        m_ref[t] = top
        l_ref[t] = jnp.sum(weights, axis=0, keepdims=True)
        acc_ref[t] = block_values(v_ref[rows, :], weights)

    def visit(slot, carry):
        t = meta_ref[1 + slot]
        peer = meta_ref[1 + slots + slot]
        rows = pl.ds(pl.multiple_of(t * tile, tile), tile)
        scores = block_scores(pk_ref[peer], q_ref[rows, :])
        old = m_ref[t]
        top = jnp.maximum(old, jnp.max(scores, axis=0, keepdims=True))
        weights = jnp.exp2((scores - top) * SCALE)
        factor = jnp.exp2((old - top) * SCALE)
        m_ref[t] = top
        l_ref[t] = l_ref[t] * factor + jnp.sum(weights, axis=0, keepdims=True)
        acc_ref[t] = acc_ref[t] * factor + block_values(pv_ref[peer], weights)
        return carry

    lax.fori_loop(0, meta_ref[0], visit, 0)
    for t in range(TILES):
        out_ref[:, pl.ds(t * tile, tile)] = (acc_ref[t] / l_ref[t]).astype(out_ref.dtype)


def attend(meta, query, key, value, incoming, chunk, heads):
    tokens = query.shape[0]
    tile = tokens // TILES
    views = incoming.shape[0]
    slots = (meta.shape[0] - 1) // 2
    own = pl.BlockSpec((tokens, HEAD_DIM), lambda h, meta: (0, chunk * heads + h))
    peer_key = pl.BlockSpec((views, tile, HEAD_DIM), lambda h, meta: (0, 0, h))
    peer_value = pl.BlockSpec((views, tile, HEAD_DIM), lambda h, meta: (0, 0, heads + h))
    blocks = heads * (TILES + min(slots, 7)) * tile * tile
    return pl.pallas_call(
        functools.partial(attend_kernel, slots, tile),
        grid_spec=pltpu.PrefetchScalarGridSpec(
            num_scalar_prefetch=1,
            grid=(heads,),
            in_specs=[own, own, own, peer_key, peer_value],
            out_specs=pl.BlockSpec((HEAD_DIM, tokens), lambda h, meta: (h, 0)),
            scratch_shapes=[
                pltpu.VMEM((TILES, 1, tile), jnp.float32),
                pltpu.VMEM((TILES, 1, tile), jnp.float32),
                pltpu.VMEM((TILES, HEAD_DIM, tile), jnp.float32),
            ],
        ),
        out_shape=jax.ShapeDtypeStruct((heads * HEAD_DIM, tokens), query.dtype),
        compiler_params=pltpu.CompilerParams(vmem_limit_bytes=40 * 2**20),
        cost_estimate=pl.CostEstimate(
            flops=blocks * HEAD_DIM * 8,
            bytes_accessed=heads * HEAD_DIM * (8 * tokens + 4 * views * tile),
            transcendentals=blocks,
        ),
    )(meta, query, key, value, incoming, incoming)


def shift(array, axis, step):
    size = lax.axis_size(axis)
    return lax.ppermute(array, axis, [(i, (i + step) % size) for i in range(size)])


def spread_weight(out_weight, after):
    views, groups = lax.axis_size("view"), lax.axis_size("head")
    view, group = lax.axis_index("view"), lax.axis_index("head")
    features = out_weight.shape[0]
    share, columns = features // views, out_weight.shape[1] // groups
    mine = lax.dynamic_slice_in_dim(out_weight, view * share, share, 0)
    rows = jnp.zeros((groups, share, columns), out_weight.dtype)
    for step in range(groups):
        to, source = (group + step) % groups, (group - step) % groups
        block = lax.dynamic_slice_in_dim(mine, to * columns, columns, 1)
        block = block if step == 0 else shift(block, "head", step)
        rows = lax.dynamic_update_index_in_dim(rows, block, source, 0)
    rows, _ = lax.optimization_barrier((rows, after))
    full = jnp.zeros((groups, features, columns), out_weight.dtype)
    for step in range(views):
        source = (view - step) % views
        block = rows if step == 0 else shift(rows, "view", step)
        full = lax.dynamic_update_slice_in_dim(full, block, source * share, 1)
    return full


def local(query, key, value, out_weight, pairs, counts):
    views = lax.axis_size("view")
    groups = lax.axis_size("head")
    me = lax.axis_index("view")
    features = query.shape[1]
    heads = features // HEAD_DIM
    chunks = heads
    per = heads // chunks
    width = per * HEAD_DIM

    slot_rows = pairs[0]
    live_count = lax.dynamic_index_in_dim(counts, me, 0, keepdims=True)
    live = jnp.arange(slot_rows.shape[0]) < live_count
    own_tiles, peers = slot_rows[:, 1], slot_rows[:, 2]
    match = (peers[:, None] == jnp.arange(views)[None, :]) & live[:, None]
    source_tiles = jnp.sum(jnp.where(match, own_tiles[:, None], 0), axis=0)
    meta = jnp.concatenate([live_count, own_tiles, peers])

    incoming = [
        lax.all_to_all(
            collect(source_tiles, key, value, c, width), "view", 0, 0, tiled=True
        )
        for c in range(chunks)
    ]
    weight = spread_weight(out_weight, incoming[min(1, chunks - 1)])

    total = None
    for c in range(chunks):
        attended = attend(meta, query, key, value, incoming[c], c, per)
        gathered = lax.all_gather(attended, "head", axis=0, tiled=False)
        gathered = gathered.reshape(groups * width, -1)
        part = weight[:, c * width : (c + 1) * width]
        term = lax.dot_general(
            part.reshape(groups * width, -1),
            gathered,
            (((0,), (0,)), ((), ())),
            preferred_element_type=jnp.float32,
        )
        total = term if total is None else total + term
    return total.astype(jnp.bfloat16)


def solution(mesh):
    placed = (
        P("view", "head"),
        P("view", "head"),
        P("view", "head"),
        P("head", None),
        P("view", None, None),
        P(),
    )
    return jax.shard_map(
        local, mesh=mesh, in_specs=placed, out_specs=P("head", "view"), check_vma=False
    )
```

```python
import functools
import math

import jax
import jax.numpy as jnp
from jax import lax
from jax.experimental import pallas as pl
from jax.experimental.pallas import tpu as pltpu
from jax.sharding import PartitionSpec as P

HEAD_DIM = 128
TILES = 4
SCALE = math.log2(math.e) / math.sqrt(HEAD_DIM)


def collect_kernel(source_ref, key_ref, value_ref, out_ref):
    width = key_ref.shape[1]
    out_ref[0, :, :width] = key_ref[...]
    out_ref[0, :, width:] = value_ref[...]


def collect(source_tiles, key, value, chunk, width):
    views = source_tiles.shape[0]
    tile = key.shape[0] // TILES
    rows = pl.BlockSpec((tile, width), lambda p, source: (source[p], chunk))
    return pl.pallas_call(
        collect_kernel,
        grid_spec=pltpu.PrefetchScalarGridSpec(
            num_scalar_prefetch=1,
            grid=(views,),
            in_specs=[rows, rows],
            out_specs=pl.BlockSpec((1, tile, 2 * width), lambda p, source: (p, 0, 0)),
        ),
        out_shape=jax.ShapeDtypeStruct((views, tile, 2 * width), key.dtype),
        compiler_params=pltpu.CompilerParams(vmem_limit_bytes=16 * 2**20),
        cost_estimate=pl.CostEstimate(
            flops=0, bytes_accessed=views * tile * width * 8, transcendentals=0
        ),
    )(source_tiles, key, value)


def block_scores(key_tile, query_tile):
    return lax.dot_general(
        key_tile, query_tile, (((1,), (1,)), ((), ())), preferred_element_type=jnp.float32
    )


def block_values(value_tile, weights):
    return lax.dot_general(
        value_tile,
        weights.astype(jnp.bfloat16),
        (((0,), (0,)), ((), ())),
        preferred_element_type=jnp.float32,
    )


def attend_kernel(
    slots, tile, meta_ref, q_ref, k_ref, v_ref, pk_ref, pv_ref, out_ref, m_ref, l_ref, acc_ref
):
    for t in range(TILES):
        rows = pl.ds(t * tile, tile)
        scores = block_scores(k_ref[rows, :], q_ref[rows, :])
        top = jnp.max(scores, axis=0, keepdims=True)
        weights = jnp.exp2((scores - top) * SCALE)
        m_ref[t] = top
        l_ref[t] = jnp.sum(weights, axis=0, keepdims=True)
        acc_ref[t] = block_values(v_ref[rows, :], weights)

    def visit(slot, carry):
        t = meta_ref[1 + slot]
        peer = meta_ref[1 + slots + slot]
        rows = pl.ds(pl.multiple_of(t * tile, tile), tile)
        scores = block_scores(pk_ref[peer], q_ref[rows, :])
        old = m_ref[t]
        top = jnp.maximum(old, jnp.max(scores, axis=0, keepdims=True))
        weights = jnp.exp2((scores - top) * SCALE)
        factor = jnp.exp2((old - top) * SCALE)
        m_ref[t] = top
        l_ref[t] = l_ref[t] * factor + jnp.sum(weights, axis=0, keepdims=True)
        acc_ref[t] = acc_ref[t] * factor + block_values(pv_ref[peer], weights)
        return carry

    lax.fori_loop(0, meta_ref[0], visit, 0)
    for t in range(TILES):
        out_ref[:, pl.ds(t * tile, tile)] = (acc_ref[t] / l_ref[t]).astype(out_ref.dtype)


def attend(meta, query, key, value, incoming, chunk, heads):
    tokens = query.shape[0]
    tile = tokens // TILES
    views = incoming.shape[0]
    slots = (meta.shape[0] - 1) // 2
    own = pl.BlockSpec((tokens, HEAD_DIM), lambda h, meta: (0, chunk + h))
    peer_key = pl.BlockSpec((views, tile, HEAD_DIM), lambda h, meta: (0, 0, h))
    peer_value = pl.BlockSpec((views, tile, HEAD_DIM), lambda h, meta: (0, 0, heads + h))
    blocks = heads * (TILES + min(slots, 7)) * tile * tile
    return pl.pallas_call(
        functools.partial(attend_kernel, slots, tile),
        grid_spec=pltpu.PrefetchScalarGridSpec(
            num_scalar_prefetch=1,
            grid=(heads,),
            in_specs=[own, own, own, peer_key, peer_value],
            out_specs=pl.BlockSpec((HEAD_DIM, tokens), lambda h, meta: (h, 0)),
            scratch_shapes=[
                pltpu.VMEM((TILES, 1, tile), jnp.float32),
                pltpu.VMEM((TILES, 1, tile), jnp.float32),
                pltpu.VMEM((TILES, HEAD_DIM, tile), jnp.float32),
            ],
        ),
        out_shape=jax.ShapeDtypeStruct((heads * HEAD_DIM, tokens), query.dtype),
        compiler_params=pltpu.CompilerParams(vmem_limit_bytes=40 * 2**20),
        cost_estimate=pl.CostEstimate(
            flops=blocks * HEAD_DIM * 8,
            bytes_accessed=heads * HEAD_DIM * (8 * tokens + 4 * views * tile),
            transcendentals=blocks,
        ),
    )(meta, query, key, value, incoming, incoming)


def shift(array, axis, step):
    size = lax.axis_size(axis)
    return lax.ppermute(array, axis, [(i, (i + step) % size) for i in range(size)])


def weight_rows(out_weight):
    groups = lax.axis_size("head")
    view, group = lax.axis_index("view"), lax.axis_index("head")
    share = out_weight.shape[0] // lax.axis_size("view")
    columns = out_weight.shape[1] // groups
    mine = lax.dynamic_slice_in_dim(out_weight, view * share, share, 0)
    blocks = []
    for step in range(groups):
        block = lax.dynamic_slice_in_dim(
            mine, lax.rem(group + step, groups) * columns, columns, 1
        )
        blocks.append(block if step == 0 else shift(block, "head", step))
    return jnp.stack(blocks)


def order_kernel(at_ref, in_ref, out_ref):
    out_ref[...] = in_ref[...]


def spread_weight(rows):
    views, groups = lax.axis_size("view"), lax.axis_size("head")
    _, share, columns = rows.shape
    stack = jnp.stack([rows] + [shift(rows, "view", step) for step in range(1, views)])
    at = jnp.stack([lax.axis_index("view"), lax.axis_index("head")])
    block = (1, 1, share, columns)
    ordered = pl.pallas_call(
        order_kernel,
        grid_spec=pltpu.PrefetchScalarGridSpec(
            num_scalar_prefetch=1,
            grid=(groups, views),
            in_specs=[
                pl.BlockSpec(
                    block,
                    lambda g, v, at: (
                        lax.rem(at[0] - v + views, views),
                        lax.rem(at[1] - g + groups, groups),
                        0,
                        0,
                    ),
                )
            ],
            out_specs=pl.BlockSpec(block, lambda g, v, at: (g, v, 0, 0)),
        ),
        out_shape=jax.ShapeDtypeStruct((groups, views, share, columns), rows.dtype),
        compiler_params=pltpu.CompilerParams(vmem_limit_bytes=16 * 2**20),
    )(at, stack)
    return ordered.reshape(groups, views * share, columns)


def local(query, key, value, out_weight, pairs, counts):
    views = lax.axis_size("view")
    groups = lax.axis_size("head")
    me = lax.axis_index("view")
    features = query.shape[1]
    heads = features // HEAD_DIM
    sizes = [1] * min(heads, 2) + [2] * ((heads - 2) // 2) + [1] * (max(heads - 2, 0) % 2)
    starts = [sum(sizes[:c]) for c in range(len(sizes))]

    slot_rows = pairs[0]
    live_count = lax.dynamic_index_in_dim(counts, me, 0, keepdims=True)
    live = jnp.arange(slot_rows.shape[0]) < live_count
    own_tiles, peers = slot_rows[:, 1], slot_rows[:, 2]
    match = (peers[:, None] == jnp.arange(views)[None, :]) & live[:, None]
    source_tiles = jnp.sum(jnp.where(match, own_tiles[:, None], 0), axis=0)
    meta = jnp.concatenate([live_count, own_tiles, peers])

    outgoing = [
        collect(source_tiles, key, value, start // size, size * HEAD_DIM)
        for start, size in zip(starts, sizes)
    ]
    rows = weight_rows(out_weight)
    if len(sizes) > 1:
        rows, outgoing[1] = lax.optimization_barrier((rows, outgoing[1]))
    incoming = [lax.all_to_all(block, "view", 0, 0, tiled=True) for block in outgoing]
    rows, incoming[-1] = lax.optimization_barrier((rows, incoming[-1]))
    weight = spread_weight(rows)

    total = None
    for start, size, block in zip(starts, sizes, incoming):
        width = size * HEAD_DIM
        attended = attend(meta, query, key, value, block, start, size)
        gathered = lax.all_gather(attended, "head", axis=0, tiled=True)
        part = weight[:, start * HEAD_DIM : start * HEAD_DIM + width]
        term = lax.dot_general(
            part.reshape(groups * width, -1),
            gathered,
            (((0,), (0,)), ((), ())),
            preferred_element_type=jnp.float32,
        )
        total = term if total is None else total + term
    return total.astype(jnp.bfloat16)


def solution(mesh):
    placed = (
        P("view", "head"),
        P("view", "head"),
        P("view", "head"),
        P("head", None),
        P("view", None, None),
        P(),
    )
    return jax.shard_map(
        local, mesh=mesh, in_specs=placed, out_specs=P("head", "view"), check_vma=False
    )
```

```python
import functools
import math

import jax
import jax.numpy as jnp
from jax import lax
from jax.experimental import pallas as pl
from jax.experimental.pallas import tpu as pltpu
from jax.sharding import PartitionSpec as P

HEAD_DIM = 128
TILES = 4
SCALE = math.log2(math.e) / math.sqrt(HEAD_DIM)


def collect_kernel(source_ref, key_ref, value_ref, out_ref):
    width = key_ref.shape[1]
    out_ref[0, :, :width] = key_ref[...]
    out_ref[0, :, width:] = value_ref[...]


def collect(source_tiles, key, value, chunk, width):
    views = source_tiles.shape[0]
    tile = key.shape[0] // TILES
    rows = pl.BlockSpec((tile, width), lambda p, source: (source[p], chunk))
    return pl.pallas_call(
        collect_kernel,
        grid_spec=pltpu.PrefetchScalarGridSpec(
            num_scalar_prefetch=1,
            grid=(views,),
            in_specs=[rows, rows],
            out_specs=pl.BlockSpec((1, tile, 2 * width), lambda p, source: (p, 0, 0)),
        ),
        out_shape=jax.ShapeDtypeStruct((views, tile, 2 * width), key.dtype),
        compiler_params=pltpu.CompilerParams(vmem_limit_bytes=16 * 2**20),
        cost_estimate=pl.CostEstimate(
            flops=0, bytes_accessed=views * tile * width * 8, transcendentals=0
        ),
    )(source_tiles, key, value)


def block_scores(key_tile, query_tile):
    return lax.dot_general(
        key_tile, query_tile, (((1,), (1,)), ((), ())), preferred_element_type=jnp.float32
    )


def block_values(value_tile, weights):
    return lax.dot_general(
        value_tile,
        weights.astype(jnp.bfloat16),
        (((0,), (0,)), ((), ())),
        preferred_element_type=jnp.float32,
    )


def attend_kernel(
    slots, tile, meta_ref, q_ref, k_ref, v_ref, pk_ref, pv_ref, out_ref, m_ref, l_ref, acc_ref
):
    for t in range(TILES):
        rows = pl.ds(t * tile, tile)
        scores = block_scores(k_ref[rows, :], q_ref[rows, :])
        top = jnp.max(scores, axis=0, keepdims=True)
        weights = jnp.exp2((scores - top) * SCALE)
        m_ref[t] = top
        l_ref[t] = jnp.sum(weights, axis=0, keepdims=True)
        acc_ref[t] = block_values(v_ref[rows, :], weights)

    def visit(slot, carry):
        t = meta_ref[1 + slot]
        peer = meta_ref[1 + slots + slot]
        rows = pl.ds(pl.multiple_of(t * tile, tile), tile)
        scores = block_scores(pk_ref[peer], q_ref[rows, :])
        old = m_ref[t]
        top = jnp.maximum(old, jnp.max(scores, axis=0, keepdims=True))
        weights = jnp.exp2((scores - top) * SCALE)
        factor = jnp.exp2((old - top) * SCALE)
        m_ref[t] = top
        l_ref[t] = l_ref[t] * factor + jnp.sum(weights, axis=0, keepdims=True)
        acc_ref[t] = acc_ref[t] * factor + block_values(pv_ref[peer], weights)
        return carry

    lax.fori_loop(0, meta_ref[0], visit, 0)
    for t in range(TILES):
        out_ref[:, pl.ds(t * tile, tile)] = (acc_ref[t] / l_ref[t]).astype(out_ref.dtype)


def attend(meta, query, key, value, incoming, chunk, heads):
    tokens = query.shape[0]
    tile = tokens // TILES
    views = incoming.shape[0]
    slots = (meta.shape[0] - 1) // 2
    own = pl.BlockSpec((tokens, HEAD_DIM), lambda h, meta: (0, chunk + h))
    peer_key = pl.BlockSpec((views, tile, HEAD_DIM), lambda h, meta: (0, 0, h))
    peer_value = pl.BlockSpec((views, tile, HEAD_DIM), lambda h, meta: (0, 0, heads + h))
    blocks = heads * (TILES + min(slots, 7)) * tile * tile
    return pl.pallas_call(
        functools.partial(attend_kernel, slots, tile),
        grid_spec=pltpu.PrefetchScalarGridSpec(
            num_scalar_prefetch=1,
            grid=(heads,),
            in_specs=[own, own, own, peer_key, peer_value],
            out_specs=pl.BlockSpec((HEAD_DIM, tokens), lambda h, meta: (h, 0)),
            scratch_shapes=[
                pltpu.VMEM((TILES, 1, tile), jnp.float32),
                pltpu.VMEM((TILES, 1, tile), jnp.float32),
                pltpu.VMEM((TILES, HEAD_DIM, tile), jnp.float32),
            ],
        ),
        out_shape=jax.ShapeDtypeStruct((heads * HEAD_DIM, tokens), query.dtype),
        compiler_params=pltpu.CompilerParams(vmem_limit_bytes=40 * 2**20),
        cost_estimate=pl.CostEstimate(
            flops=blocks * HEAD_DIM * 8,
            bytes_accessed=heads * HEAD_DIM * (8 * tokens + 4 * views * tile),
            transcendentals=blocks,
        ),
    )(meta, query, key, value, incoming, incoming)


def shift(array, axis, step):
    size = lax.axis_size(axis)
    return lax.ppermute(array, axis, [(i, (i + step) % size) for i in range(size)])


def weight_rows(out_weight):
    groups = lax.axis_size("head")
    view, group = lax.axis_index("view"), lax.axis_index("head")
    pair = math.gcd(lax.axis_size("view"), 2)
    share = out_weight.shape[0] // pair
    columns = out_weight.shape[1] // groups
    mine = lax.dynamic_slice_in_dim(out_weight, lax.rem(view, pair) * share, share, 0)
    blocks = []
    for step in range(groups):
        block = lax.dynamic_slice_in_dim(
            mine, lax.rem(group + step, groups) * columns, columns, 1
        )
        blocks.append(block if step == 0 else shift(block, "head", step))
    return jnp.stack(blocks)


def order_kernel(at_ref, in_ref, out_ref):
    out_ref[...] = in_ref[...]


def spread_weight(rows):
    views, groups = lax.axis_size("view"), lax.axis_size("head")
    pair = math.gcd(views, 2)
    _, share, columns = rows.shape
    parts = [rows]
    if pair == 2:
        parts.append(lax.ppermute(rows, "view", [(i, i ^ 1) for i in range(views)]))
    stack = jnp.stack(parts)
    at = jnp.stack([lax.rem(lax.axis_index("view"), pair), lax.axis_index("head")])
    block = (1, 1, share, columns)
    ordered = pl.pallas_call(
        order_kernel,
        grid_spec=pltpu.PrefetchScalarGridSpec(
            num_scalar_prefetch=1,
            grid=(groups, pair),
            in_specs=[
                pl.BlockSpec(
                    block,
                    lambda g, v, at: (
                        lax.rem(at[0] - v + pair, pair),
                        lax.rem(at[1] - g + groups, groups),
                        0,
                        0,
                    ),
                )
            ],
            out_specs=pl.BlockSpec(block, lambda g, v, at: (g, v, 0, 0)),
        ),
        out_shape=jax.ShapeDtypeStruct((groups, pair, share, columns), rows.dtype),
        compiler_params=pltpu.CompilerParams(vmem_limit_bytes=16 * 2**20),
    )(at, stack)
    return ordered.reshape(groups, pair * share, columns)


def local(query, key, value, out_weight, pairs, counts):
    views = lax.axis_size("view")
    groups = lax.axis_size("head")
    me = lax.axis_index("view")
    features = query.shape[1]
    heads = features // HEAD_DIM
    sizes = [1] * min(heads, 2) + [2] * ((heads - 2) // 2) + [1] * (max(heads - 2, 0) % 2)
    starts = [sum(sizes[:c]) for c in range(len(sizes))]

    slot_rows = pairs[0]
    live_count = lax.dynamic_index_in_dim(counts, me, 0, keepdims=True)
    live = jnp.arange(slot_rows.shape[0]) < live_count
    own_tiles, peers = slot_rows[:, 1], slot_rows[:, 2]
    match = (peers[:, None] == jnp.arange(views)[None, :]) & live[:, None]
    source_tiles = jnp.sum(jnp.where(match, own_tiles[:, None], 0), axis=0)
    meta = jnp.concatenate([live_count, own_tiles, peers])

    outgoing = [
        collect(source_tiles, key, value, start // size, size * HEAD_DIM)
        for start, size in zip(starts, sizes)
    ]
    rows = weight_rows(out_weight)
    incoming = [lax.all_to_all(block, "view", 0, 0, tiled=True) for block in outgoing]
    rows, incoming[0] = lax.optimization_barrier((rows, incoming[0]))
    weight = spread_weight(rows)

    total = None
    for start, size, block in zip(starts, sizes, incoming):
        width = size * HEAD_DIM
        attended = attend(meta, query, key, value, block, start, size)
        gathered = lax.all_gather(attended, "head", axis=0, tiled=True)
        part = weight[:, start * HEAD_DIM : start * HEAD_DIM + width]
        term = lax.dot_general(
            part.reshape(groups * width, -1),
            gathered,
            (((0,), (0,)), ((), ())),
            preferred_element_type=jnp.float32,
        )
        total = term if total is None else total + term
    return total.astype(jnp.bfloat16)


def solution(mesh):
    placed = (
        P("view", "head"),
        P("view", "head"),
        P("view", "head"),
        P("head", None),
        P("view", None, None),
        P(),
    )
    return jax.shard_map(
        local, mesh=mesh, in_specs=placed, out_specs=P("head", "view"), check_vma=False
    )
```

```python
import functools
import math

import jax
import jax.numpy as jnp
from jax import lax
from jax.experimental import pallas as pl
from jax.experimental.pallas import tpu as pltpu
from jax.sharding import PartitionSpec as P

HEAD_DIM = 128
TILES = 4
SCALE = math.log2(math.e) / math.sqrt(HEAD_DIM)


def collect_kernel(source_ref, key_ref, value_ref, out_ref):
    width = key_ref.shape[1]
    out_ref[0, :, :width] = key_ref[...]
    out_ref[0, :, width:] = value_ref[...]


def collect(source_tiles, key, value, chunk, width):
    views = source_tiles.shape[0]
    tile = key.shape[0] // TILES
    rows = pl.BlockSpec((tile, width), lambda p, source: (source[p], chunk))
    return pl.pallas_call(
        collect_kernel,
        grid_spec=pltpu.PrefetchScalarGridSpec(
            num_scalar_prefetch=1,
            grid=(views,),
            in_specs=[rows, rows],
            out_specs=pl.BlockSpec((1, tile, 2 * width), lambda p, source: (p, 0, 0)),
        ),
        out_shape=jax.ShapeDtypeStruct((views, tile, 2 * width), key.dtype),
        compiler_params=pltpu.CompilerParams(vmem_limit_bytes=16 * 2**20),
        cost_estimate=pl.CostEstimate(
            flops=0, bytes_accessed=views * tile * width * 8, transcendentals=0
        ),
    )(source_tiles, key, value)


def block_scores(key_tile, query_tile):
    return lax.dot_general(
        key_tile, query_tile, (((1,), (1,)), ((), ())), preferred_element_type=jnp.float32
    )


def block_values(value_tile, weights):
    return lax.dot_general(
        value_tile,
        weights.astype(jnp.bfloat16),
        (((0,), (0,)), ((), ())),
        preferred_element_type=jnp.float32,
    )


def attend_kernel(
    slots, tile, meta_ref, q_ref, k_ref, v_ref, pk_ref, pv_ref, out_ref, m_ref, l_ref, acc_ref
):
    for t in range(TILES):
        rows = pl.ds(t * tile, tile)
        scores = block_scores(k_ref[rows, :], q_ref[rows, :])
        top = jnp.max(scores, axis=0, keepdims=True)
        weights = jnp.exp2((scores - top) * SCALE)
        m_ref[t] = top
        l_ref[t] = jnp.sum(weights, axis=0, keepdims=True)
        acc_ref[t] = block_values(v_ref[rows, :], weights)

    def visit(slot, carry):
        t = meta_ref[1 + slot]
        peer = meta_ref[1 + slots + slot]
        rows = pl.ds(pl.multiple_of(t * tile, tile), tile)
        scores = block_scores(pk_ref[peer], q_ref[rows, :])
        old = m_ref[t]
        top = jnp.maximum(old, jnp.max(scores, axis=0, keepdims=True))
        weights = jnp.exp2((scores - top) * SCALE)
        factor = jnp.exp2((old - top) * SCALE)
        m_ref[t] = top
        l_ref[t] = l_ref[t] * factor + jnp.sum(weights, axis=0, keepdims=True)
        acc_ref[t] = acc_ref[t] * factor + block_values(pv_ref[peer], weights)
        return carry

    lax.fori_loop(0, meta_ref[0], visit, 0)
    for t in range(TILES):
        out_ref[:, pl.ds(t * tile, tile)] = (acc_ref[t] / l_ref[t]).astype(out_ref.dtype)


def attend(meta, query, key, value, incoming, chunk, heads):
    tokens = query.shape[0]
    tile = tokens // TILES
    views = incoming.shape[0]
    slots = (meta.shape[0] - 1) // 2
    own = pl.BlockSpec((tokens, HEAD_DIM), lambda h, meta: (0, chunk + h))
    peer_key = pl.BlockSpec((views, tile, HEAD_DIM), lambda h, meta: (0, 0, h))
    peer_value = pl.BlockSpec((views, tile, HEAD_DIM), lambda h, meta: (0, 0, heads + h))
    blocks = heads * (TILES + min(slots, 7)) * tile * tile
    return pl.pallas_call(
        functools.partial(attend_kernel, slots, tile),
        grid_spec=pltpu.PrefetchScalarGridSpec(
            num_scalar_prefetch=1,
            grid=(heads,),
            in_specs=[own, own, own, peer_key, peer_value],
            out_specs=pl.BlockSpec((HEAD_DIM, tokens), lambda h, meta: (h, 0)),
            scratch_shapes=[
                pltpu.VMEM((TILES, 1, tile), jnp.float32),
                pltpu.VMEM((TILES, 1, tile), jnp.float32),
                pltpu.VMEM((TILES, HEAD_DIM, tile), jnp.float32),
            ],
        ),
        out_shape=jax.ShapeDtypeStruct((heads * HEAD_DIM, tokens), query.dtype),
        compiler_params=pltpu.CompilerParams(vmem_limit_bytes=40 * 2**20),
        cost_estimate=pl.CostEstimate(
            flops=blocks * HEAD_DIM * 8,
            bytes_accessed=heads * HEAD_DIM * (8 * tokens + 4 * views * tile),
            transcendentals=blocks,
        ),
    )(meta, query, key, value, incoming, incoming)


def shift(array, axis, step):
    size = lax.axis_size(axis)
    return lax.ppermute(array, axis, [(i, (i + step) % size) for i in range(size)])


def weight_rows(out_weight):
    groups = lax.axis_size("head")
    view, group = lax.axis_index("view"), lax.axis_index("head")
    share = out_weight.shape[0] // lax.axis_size("view")
    columns = out_weight.shape[1] // groups
    mine = lax.dynamic_slice_in_dim(out_weight, view * share, share, 0)
    blocks = []
    for step in range(groups):
        block = lax.dynamic_slice_in_dim(
            mine, lax.rem(group + step, groups) * columns, columns, 1
        )
        blocks.append(block if step == 0 else shift(block, "head", step))
    return jnp.stack(blocks)


def order_kernel(at_ref, in_ref, out_ref):
    out_ref[...] = in_ref[...]


def spread_weight(rows):
    views, groups = lax.axis_size("view"), lax.axis_size("head")
    _, share, columns = rows.shape
    stack = jnp.stack([rows] + [shift(rows, "view", step) for step in range(1, views)])
    at = jnp.stack([lax.axis_index("view"), lax.axis_index("head")])
    block = (1, 1, share, columns)
    ordered = pl.pallas_call(
        order_kernel,
        grid_spec=pltpu.PrefetchScalarGridSpec(
            num_scalar_prefetch=1,
            grid=(groups, views),
            in_specs=[
                pl.BlockSpec(
                    block,
                    lambda g, v, at: (
                        lax.rem(at[0] - v + views, views),
                        lax.rem(at[1] - g + groups, groups),
                        0,
                        0,
                    ),
                )
            ],
            out_specs=pl.BlockSpec(block, lambda g, v, at: (g, v, 0, 0)),
        ),
        out_shape=jax.ShapeDtypeStruct((groups, views, share, columns), rows.dtype),
        compiler_params=pltpu.CompilerParams(vmem_limit_bytes=16 * 2**20),
    )(at, stack)
    return ordered.reshape(groups, views * share, columns)


def local(query, key, value, out_weight, pairs, counts):
    views = lax.axis_size("view")
    groups = lax.axis_size("head")
    me = lax.axis_index("view")
    features = query.shape[1]
    heads = features // HEAD_DIM
    sizes = [1] * min(heads, 2) + [2] * ((heads - 2) // 2) + [1] * (max(heads - 2, 0) % 2)
    starts = [sum(sizes[:c]) for c in range(len(sizes))]

    slot_rows = pairs[0]
    live_count = lax.dynamic_index_in_dim(counts, me, 0, keepdims=True)
    live = jnp.arange(slot_rows.shape[0]) < live_count
    own_tiles, peers = slot_rows[:, 1], slot_rows[:, 2]
    match = (peers[:, None] == jnp.arange(views)[None, :]) & live[:, None]
    source_tiles = jnp.sum(jnp.where(match, own_tiles[:, None], 0), axis=0)
    meta = jnp.concatenate([live_count, own_tiles, peers])

    outgoing = [
        collect(source_tiles, key, value, start // size, size * HEAD_DIM)
        for start, size in zip(starts, sizes)
    ]
    rows = weight_rows(out_weight)
    incoming = [lax.all_to_all(block, "view", 0, 0, tiled=True) for block in outgoing]
    rows, incoming[0] = lax.optimization_barrier((rows, incoming[0]))
    rows, incoming[-1] = lax.optimization_barrier((rows, incoming[-1]))
    weight = spread_weight(rows)

    total = None
    for start, size, block in zip(starts, sizes, incoming):
        width = size * HEAD_DIM
        attended = attend(meta, query, key, value, block, start, size)
        gathered = lax.all_gather(attended, "head", axis=0, tiled=True)
        part = weight[:, start * HEAD_DIM : start * HEAD_DIM + width]
        term = lax.dot_general(
            part.reshape(groups * width, -1),
            gathered,
            (((0,), (0,)), ((), ())),
            preferred_element_type=jnp.float32,
        )
        total = term if total is None else total + term
    return total.astype(jnp.bfloat16)


def solution(mesh):
    placed = (
        P("view", "head"),
        P("view", "head"),
        P("view", "head"),
        P("head", None),
        P("view", None, None),
        P(),
    )
    return jax.shard_map(
        local, mesh=mesh, in_specs=placed, out_specs=P("head", "view"), check_vma=False
    )
```
